32 devices in a mesh: dp: 16 (over z, x, core), tensor: 2 (over y).
Axes of the slice: x: 2, y: 2, z: 4, core: 2. Of those that a mesh axis runs over, the one named last changes fastest.
Arguments:
- tokens: bfloat16 [16384, 1024], P(('dp', 'tensor')), may hold values from -6 to 6
- gains: float32 [2, 1024], replicated, may hold values from 0.5 to 1.5
- shifts: float32 [4, 1024], replicated, may hold values from -1.8 to 1.8
- w_qkv: bfloat16 [1024, 3, 1024], P('dp', None, 'tensor'), may hold values from -0.1875 to 0.1875
- bias_qv: float32 [2, 1024], P(None, 'tensor'), may hold values from -1.8 to 1.8
- w_out: bfloat16 [1024, 1024], P('tensor', 'dp'), may hold values from -1 to 1
- w_in: bfloat16 [1024, 4096], P('dp', 'tensor'), may hold values from -0.1875 to 0.1875
- bias_in: float32 [4096], P('tensor'), may hold values from -1.8 to 1.8
- w_down: bfloat16 [4096, 1024], P('tensor', 'dp'), may hold values from -0.09375 to 0.09375
- segments: int32 [16, 1024], P('dp'), may hold values from 0 to 2, never falling along the last dimension, each value on 1 to 512 neighbouring positions
- grad_output: bfloat16 [16384, 1024], P(('dp', 'tensor')), may hold values from -6 to 6
Outputs:
- output: bfloat16 [16384, 1024], P(('dp', 'tensor'))
- input_grad: bfloat16 [16384, 1024], P(('dp', 'tensor'))
- gains_grad: float32 [2, 1024], P(None, ('dp', 'tensor'))
- shifts_grad: float32 [4, 1024], P(None, ('dp', 'tensor'))
- w_qkv_grad: float32 [1024, 3, 1024], P('dp', None, 'tensor')
- bias_qv_grad: float32 [2, 1024], P(None, ('tensor', 'dp'))
- w_out_grad: float32 [1024, 1024], P('tensor', 'dp')
- w_in_grad: float32 [1024, 4096], P('dp', 'tensor')
- bias_in_grad: float32 [4096], P(('tensor', 'dp'))
- w_down_grad: float32 [4096, 1024], P('tensor', 'dp')
The draws below stay inside these ranges and needn't reach their ends.
Inputs may be any that keep to these rules, and one draw needn't show every extreme that they name: `segments`: along each sequence the numbers never fall; each document spans 1 to 512 tokens.
All inputs are finite; a program needn't handle non-finite values.
Results may differ from the reference program's by a relative error of at most 0.02.
Values may be sent and summed in bfloat16 or wider, within the bound.
A program may use at most 192 MiB of HBM per device.

```python
import math
import jax
import jax.numpy as jnp
import numpy as np
from jax import lax

D = 1024
HEADS = 16
HEAD_DIM = 64
FF = 4096
SEQ_LEN = 1024
DOCS = 3
DOC_MAX = 512
SEQ_DEV = 1
SEQS = 16
TOKENS = 16384
N_DP = 16


def block_levels(rng, dims, split, smallest, high):
    def one(axis_at, shards_of):
        heights = jax.random.uniform(jax.random.fold_in(jax.random.fold_in(rng, 6), axis_at), (shards_of,), jnp.float32, smallest / len(split), high / len(split))
        return jnp.repeat(jnp.exp(heights), dims[axis_at] // shards_of).reshape((-1,) + (1,) * (len(dims) - axis_at - 1))

    level = one(*split[0])
    for cut in split[1:]:
        level = level * one(*cut)
    return level


def split_up(number_of, total, bound, skew):
    weights = [(1 << 20) // math.isqrt(standing ** skew) + 1 for standing in range(2, number_of + 1)]
    rest, counts = total - bound - (number_of - 1), [1] * (number_of - 1)
    while rest > 0:
        free = [i for i in range(number_of - 1) if counts[i] < bound]
        pool, remaining = sum([weights[i] for i in free]), rest
        for i in free:
            more = min(bound - counts[i], max(1, remaining * weights[i] // pool), rest)
            counts[i] = counts[i] + more
            rest = rest - more
    return np.array([bound] + counts)


def uneven_parts(stream_key, amount, total, bound, lean):
    if amount == 2:
        one = jax.random.randint(stream_key, (), max(1, total - bound), min(bound, total - 1) + 1)
        return jnp.stack([one, total - one])
    tallies = jnp.asarray(split_up(amount, total, bound, lean), jnp.int32)
    twos = (amount - 1) // 2
    source_of, receiver = tallies[1:1 + 2 * twos:2], tallies[2:2 + 2 * twos:2]
    room = jnp.minimum(source_of - 1, bound - receiver)
    moved = jax.random.randint(jax.random.fold_in(stream_key, 1), (twos,), 0, 1 << 20) % (room + 1)
    tallies = tallies.at[1:1 + 2 * twos:2].set(source_of - moved).at[2:2 + 2 * twos:2].set(receiver + moved)
    return tallies[jax.random.permutation(jax.random.fold_in(stream_key, 2), amount)]


def normal_values(rng, extent, deviation, bound, pieces=(), kind=jnp.bfloat16):
    values = jax.random.normal(rng, extent, jnp.float32) * deviation
    if len(pieces) > 0:
        values = block_levels(rng, extent, pieces, -0.22, 0.18) * values
    return jnp.clip(values, min=-bound, max=bound).astype(kind)


def setup_inputs(seed: int = 0) -> dict:
    key_of = jax.random.split(jax.random.key(seed), 12)
    tokens = normal_values(key_of[0], (TOKENS, D), 1.0, 6.0, ((0, 32),))
    gains = jnp.clip(1.0 + 0.1 * jax.random.normal(key_of[1], (2, D), jnp.float32), 0.5, 1.5)
    shifts = normal_values(key_of[2], (4, D), 0.3, 1.8, (), jnp.float32)
    w_qkv = normal_values(key_of[3], (D, 3, D), D ** -0.5, 0.1875, ((0, 16), (2, 2)))
    bias_qv = normal_values(key_of[4], (2, D), 0.3, 1.8, ((1, 2),), jnp.float32)
    w_out = normal_values(key_of[5], (D, D), (D // 32) ** -0.5, 1.0, ((0, 2), (1, 16)))
    w_in = normal_values(key_of[6], (D, FF), D ** -0.5, 0.1875, ((0, 16), (1, 2)))
    bias_in = normal_values(key_of[7], (FF,), 0.3, 1.8, ((0, 2),), jnp.float32)
    w_down = normal_values(key_of[8], (FF, D), FF ** -0.5, 0.09375, ((0, 2), (1, 16)))
    segments = jax.vmap(lambda own: jnp.searchsorted(jnp.cumsum(uneven_parts(own, DOCS, SEQ_LEN, DOC_MAX, 0)), jnp.arange(SEQ_LEN), side="right"))(jax.random.split(key_of[9], SEQS)).reshape((SEQS, SEQ_LEN)).astype(jnp.int32)
    grad_output = normal_values(key_of[10], (TOKENS, D), 1.0, 6.0, ((0, 32),))
    return {"tokens": tokens, "gains": gains, "shifts": shifts, "w_qkv": w_qkv, "bias_qv": bias_qv, "w_out": w_out, "w_in": w_in, "bias_in": bias_in, "w_down": w_down, "segments": segments, "grad_output": grad_output}


EPS = 1e-05
MASKED = -1000000000.0
GELU_C = 0.7978845608028654
HIGHEST = lax.Precision.HIGHEST

@jax.custom_vjp
def low(v):
    return lax.optimization_barrier(v.astype(jnp.bfloat16)).astype(jnp.float32)

@jax.custom_vjp
def low_back(v):
    return v

def low_keep(v):
    return (low(v), None)

def low_pass(kept, grad):
    return (grad,)

def back_keep(v):
    return (v, None)

def back_low(kept, grad):
    return (low(grad),)
low.defvjp(low_keep, low_pass)
low_back.defvjp(back_keep, back_low)

def layer_norm(value, gain, shift):
    centre = value - lax.optimization_barrier(jnp.mean(value, axis=-1, keepdims=True))
    spread = lax.optimization_barrier(jnp.mean(centre * centre, axis=-1, keepdims=True))
    return centre * lax.rsqrt(spread + EPS) * gain + shift

def gelu_tanh(value):
    return 0.5 * value * (1.0 + jnp.tanh(GELU_C * (value + 0.044715 * value * value * value)))

def attend(query, key, value, seg):
    length = query.shape[0]
    block = min(512, length)
    scale = 1.0 / math.sqrt(HEAD_DIM)
    key_pos = jnp.arange(length, dtype=jnp.int32)

    def one_block(start):
        q_rows = lax.dynamic_slice_in_dim(query, start, block, 0)
        seg_rows = lax.dynamic_slice_in_dim(seg, start, block, 0)
        row_pos = start + jnp.arange(block, dtype=jnp.int32)
        allowed = (seg_rows[:, None] == seg[None, :]) & (row_pos[:, None] >= key_pos[None, :])
        scores = jnp.einsum('qhd,khd->hqk', q_rows, key, precision=HIGHEST) * scale
        scores = low_back(scores)
        scores = jnp.where(allowed[None], scores, MASKED)
        top = lax.optimization_barrier(jnp.max(scores, axis=-1, keepdims=True))
        expo = jnp.exp(scores - top)
        probs = low(expo / lax.optimization_barrier(jnp.sum(expo, axis=-1, keepdims=True)))
        return jnp.einsum('hqk,khd->qhd', probs, value, precision=HIGHEST)
    starts = (jnp.arange(length // block, dtype=jnp.int32) * block).astype(jnp.int32)
    blocks = lax.map(jax.checkpoint(one_block), starts)
    return blocks.reshape(length, HEADS, HEAD_DIM)

def forward(rows, gains, shifts, w_qkv, bias_qv, w_out, w_in, bias_in, w_down, seg):
    total = rows.shape[0]
    normed = low(layer_norm(rows, gains[0], shifts[0]))
    mixed = jnp.einsum('td,dcn->tcn', normed, w_qkv, precision=HIGHEST)
    mixed = mixed + jnp.stack([bias_qv[0], jnp.zeros_like(bias_qv[0]), bias_qv[1]])[None]
    mixed = low(low_back(mixed))
    shaped = mixed.reshape(SEQ_DEV, SEQ_LEN, 3, HEADS, HEAD_DIM)

    def per_seq(items):
        return attend(items[0], items[1], items[2], items[3])
    attended = lax.map(per_seq, (shaped[:, :, 0], shaped[:, :, 1], shaped[:, :, 2], seg))
    attended = low(low_back(attended.reshape(total, D)))
    branch = low_back(jnp.dot(attended, w_out, precision=HIGHEST) + shifts[1])
    middle = rows + branch
    normed_two = low(layer_norm(middle, gains[1], shifts[2]))
    hidden = low_back(jnp.dot(normed_two, w_in, precision=HIGHEST) + bias_in)
    hidden = low(gelu_tanh(hidden))
    return middle + jnp.dot(hidden, w_down, precision=HIGHEST) + shifts[3]

def reference(tokens, gains, shifts, w_qkv, bias_qv, w_out, w_in, bias_in, w_down, segments, grad_output):
    params = (gains.astype(jnp.float32), shifts.astype(jnp.float32), w_qkv.astype(jnp.float32), bias_qv.astype(jnp.float32), w_out.astype(jnp.float32), w_in.astype(jnp.float32), bias_in.astype(jnp.float32), w_down.astype(jnp.float32))
    group = SEQ_DEV * SEQ_LEN
    rows_all = tokens.astype(jnp.float32).reshape(N_DP, group, D)
    cot_all = grad_output.astype(jnp.float32).reshape(N_DP, group, D)
    seg_all = segments.reshape(N_DP, SEQ_DEV, SEQ_LEN)

    def step(accum, items):
        rows, cot, seg = items

        def local(rows_in, *weights):
            return forward(rows_in, *weights, seg)
        result, back = jax.vjp(local, rows, *params)
        grads = back(cot)
        accum = tuple((prior + fresh for prior, fresh in zip(accum, grads[1:])))
        return (accum, (result.astype(jnp.bfloat16), grads[0].astype(jnp.bfloat16)))
    start = tuple((jnp.zeros_like(weight) for weight in params))
    accum, pair = lax.scan(step, start, (rows_all, cot_all, seg_all))
    return (pair[0].reshape(TOKENS, D), pair[1].reshape(TOKENS, D), accum[0], accum[1], accum[2], accum[3], accum[4], accum[5], accum[6], accum[7])
```

```python
import math

import jax
import jax.numpy as jnp
from jax import lax
from jax.sharding import PartitionSpec as P

HEAD_DIM = 64


EPS = 1e-05
MASKED = -1000000000.0
GELU_C = 0.7978845608028654


def layer_norm(value, gain, shift):
    centre = value - jnp.mean(value, axis=-1, keepdims=True)
    spread = jnp.mean(centre * centre, axis=-1, keepdims=True)
    return centre * lax.rsqrt(spread + EPS) * gain + shift


def gelu_tanh(value):
    return 0.5 * value * (1.0 + jnp.tanh(GELU_C * (value + 0.044715 * value * value * value)))


def xor_send(value, axis, distance):
    size = lax.axis_size(axis)
    return lax.ppermute(value, axis, [(i, i ^ distance) for i in range(size)])


def join_shards(*shards):
    widths = [shard.shape[1] for shard in shards]
    full = lax.all_gather(jnp.concatenate(shards, axis=1), "dp", axis=0, tiled=True)
    parts = []
    start = 0
    for width in widths:
        parts.append(full[:, start : start + width])
        start += width
    return parts


def spread_rows(rows):
    blocks = [rows] + [xor_send(rows, "tensor", d) for d in range(1, lax.axis_size("tensor"))]
    return jnp.concatenate(blocks, axis=0)


def to_natural(values):
    ranks = lax.axis_size("tensor")
    me = lax.axis_index("tensor")
    rows = values.shape[0] // ranks
    if ranks == 2:
        own, other = values[:rows], values[rows:]
        return jnp.concatenate(
            [jnp.where(me == 0, own, other), jnp.where(me == 0, other, own)], axis=0
        )
    blocks = values.reshape(ranks, rows, *values.shape[1:])
    picked = [
        lax.dynamic_index_in_dim(blocks, jnp.bitwise_xor(me, j), 0, keepdims=False)
        for j in range(ranks)
    ]
    return jnp.concatenate(picked, axis=0)


def sum_to_owner(product, values):
    ranks = lax.axis_size("tensor")
    rows = values.shape[0] // ranks
    arrived = []
    for distance in range(1, ranks):
        part = product(values[distance * rows : (distance + 1) * rows]).astype(jnp.bfloat16)
        arrived.append(xor_send(part, "tensor", distance))
    total = product(values[:rows])
    for part in arrived:
        total = total + part.astype(jnp.float32)
    return total


def times(weight):
    return lambda rows: jnp.dot(rows, weight, preferred_element_type=jnp.float32)


def times_transposed(weight):
    return lambda rows: lax.dot_general(
        rows, weight, (((1,), (1,)), ((), ())), preferred_element_type=jnp.float32
    )


def halving_sum(value, axis, order, keep_dtype):
    size = lax.axis_size(axis)
    me = lax.axis_index(axis)
    left = [bit for bit in reversed(range(len(order)))]
    tail = (value.shape[0] // size,) + value.shape[1:]
    value = value.reshape((2,) * len(order) + tail)
    for step, bit in enumerate(order):
        place = left.index(bit)
        left.remove(bit)
        mine = lax.rem(me // (1 << bit), 2)
        send = lax.dynamic_index_in_dim(value, 1 - mine, place, keepdims=False)
        keep = lax.dynamic_index_in_dim(value, mine, place, keepdims=False)
        got = xor_send(send, axis, 1 << bit)
        value = keep.astype(jnp.float32) + got.astype(jnp.float32)
        if step < len(order) - 1:
            value = value.astype(keep_dtype)
    return value


def dp_orders():
    bits = lax.axis_size("dp").bit_length() - 1
    ahead = list(range(bits))
    return ahead, [0] + ahead[2:] + ahead[1:2]


def dp_sum(value, order):
    return halving_sum(value.astype(jnp.bfloat16), "dp", order, jnp.bfloat16)


def masks_for(seg, start, end):
    positions = jnp.arange(end, dtype=jnp.int32)
    same = seg[start:end, None] == seg[None, :end]
    causal = positions[start:end, None] >= positions[None, :end]
    return same & causal


def attention_forward(query, key, value, segments, scale):
    length = query.shape[1]
    block = min(512, length)
    blocks = length // block

    def one_seq(items):
        q_seq, k_seq, v_seq, seg = items
        outs = []
        sums = []
        for index in range(blocks):
            start = index * block
            end = start + block
            allowed = masks_for(seg, start, end)
            scores = (
                jnp.einsum(
                    "qhd,khd->hqk",
                    q_seq[start:end],
                    k_seq[:end],
                    preferred_element_type=jnp.float32,
                )
                * scale
            )
            scores = jnp.where(allowed[None], scores, MASKED)
            top = jnp.max(scores, axis=-1, keepdims=True)
            expo = jnp.exp(scores - top)
            total = jnp.sum(expo, axis=-1, keepdims=True)
            probs = (expo / total).astype(jnp.bfloat16)
            outs.append(
                jnp.einsum("hqk,khd->qhd", probs, v_seq[:end], preferred_element_type=jnp.float32)
            )
            sums.append((top + jnp.log(total))[..., 0])
        return (jnp.concatenate(outs, 0), jnp.concatenate(sums, 1))

    return lax.map(one_seq, (query, key, value, segments))


def attention_backward(query, key, value, segments, logsum, grad_att, scale):
    length = query.shape[1]
    block = min(512, length)
    blocks = length // block

    def one_seq(items):
        q_seq, k_seq, v_seq, seg, lse, do_seq = items
        dq_parts = []
        key_grad = jnp.zeros(k_seq.shape, jnp.float32)
        value_grad = jnp.zeros(v_seq.shape, jnp.float32)
        for index in range(blocks):
            start = index * block
            end = start + block
            allowed = masks_for(seg, start, end)
            q_rows = q_seq[start:end]
            do_rows = do_seq[start:end]
            scores = (
                jnp.einsum("qhd,khd->hqk", q_rows, k_seq[:end], preferred_element_type=jnp.float32)
                * scale
            )
            scores = jnp.where(allowed[None], scores, MASKED)
            probs = jnp.exp(scores - lse[:, start:end, None])
            probs_low = probs.astype(jnp.bfloat16)
            dprobs = jnp.einsum(
                "qhd,khd->hqk", do_rows, v_seq[:end], preferred_element_type=jnp.float32
            )
            inner = jnp.sum(dprobs * probs, axis=-1, keepdims=True)
            dscores = (probs * (dprobs - inner)).astype(jnp.bfloat16)
            dq_parts.append(
                jnp.einsum("hqk,khd->qhd", dscores, k_seq[:end], preferred_element_type=jnp.float32)
                * scale
            )
            key_grad = key_grad.at[:end].add(
                jnp.einsum("hqk,qhd->khd", dscores, q_rows, preferred_element_type=jnp.float32)
                * scale
            )
            value_grad = value_grad.at[:end].add(
                jnp.einsum("hqk,qhd->khd", probs_low, do_rows, preferred_element_type=jnp.float32)
            )
        return (jnp.concatenate(dq_parts, 0), key_grad, value_grad)

    return lax.map(one_seq, (query, key, value, segments, logsum, grad_att))


def per_device(
    tokens, gains, shifts, w_qkv, bias_qv, w_out, w_in, bias_in, w_down, segments, grad_output
):
    seqs, length = segments.shape
    scale = 1.0 / math.sqrt(HEAD_DIM)
    order_a, order_b = dp_orders()
    shard = w_qkv.shape[0]
    local_width = w_qkv.shape[2]
    ranks = lax.axis_size("tensor")
    my_rank = lax.axis_index("tensor")
    rows_local = tokens.shape[0]
    qkv_flat, out_turned = join_shards(w_qkv.reshape(shard, 3 * local_width), w_out.T)
    in_full, down_turned = join_shards(w_in, w_down.T)
    heads = local_width // HEAD_DIM
    rows_in = tokens.astype(jnp.float32)
    normed_one = layer_norm(rows_in, gains[0], shifts[0])
    full_a = spread_rows(normed_one.astype(jnp.bfloat16))
    full_dy = spread_rows(grad_output)
    total = full_a.shape[0]
    bias_all = jnp.concatenate([bias_qv[0], jnp.zeros_like(bias_qv[0]), bias_qv[1]])
    mixed = jnp.dot(full_a, qkv_flat, preferred_element_type=jnp.float32) + bias_all
    shaped = to_natural(mixed.astype(jnp.bfloat16)).reshape(seqs, length, 3, heads, HEAD_DIM)
    query = shaped[:, :, 0]
    key = shaped[:, :, 1]
    value = shaped[:, :, 2]
    attended, logsum = attention_forward(query, key, value, segments, scale)
    attended_low = to_natural(attended.reshape(total, local_width).astype(jnp.bfloat16))
    middle = rows_in + sum_to_owner(times_transposed(out_turned), attended_low) + shifts[1]
    normed_two = layer_norm(middle, gains[1], shifts[2])
    full_m = spread_rows(normed_two.astype(jnp.bfloat16))
    hidden_grad = jnp.dot(full_dy, down_turned, preferred_element_type=jnp.float32)
    hidden_pre = jnp.dot(full_m, in_full, preferred_element_type=jnp.float32) + bias_in
    hidden_low = gelu_tanh(hidden_pre).astype(jnp.bfloat16)
    gelu_out, gelu_back = jax.vjp(gelu_tanh, hidden_pre)
    pre_grad = gelu_back(hidden_grad)[0].astype(jnp.bfloat16)
    normed_two_grad = sum_to_owner(times_transposed(in_full), pre_grad)
    result = middle + sum_to_owner(times_transposed(down_turned), hidden_low) + shifts[3]
    output = result.astype(jnp.bfloat16)
    grad_rows = grad_output.astype(jnp.float32)
    bias_in_part = jnp.sum(pre_grad, axis=0, dtype=jnp.float32)
    down_grad = lax.dot_general(
        full_dy, hidden_low, (((0,), (0,)), ((), ())), preferred_element_type=jnp.float32
    )
    in_grad = lax.dot_general(
        full_m, pre_grad, (((0,), (0,)), ((), ())), preferred_element_type=jnp.float32
    )
    ff_in = dp_sum(in_grad, order_a)
    ff_down = dp_sum(down_grad, order_b).T
    norm_two_out, norm_two_back = jax.vjp(layer_norm, middle, gains[1], shifts[2])
    middle_part, gain_two_grad, shift_two_grad = norm_two_back(normed_two_grad)
    middle_grad = grad_rows + middle_part
    branch_low = middle_grad.astype(jnp.bfloat16)
    full_branch = spread_rows(branch_low)
    attended_grad = jnp.dot(full_branch, out_turned, preferred_element_type=jnp.float32)
    attended_grad_low = to_natural(attended_grad.astype(jnp.bfloat16))
    out_grad = lax.dot_general(
        full_branch, attended_low, (((0,), (0,)), ((), ())), preferred_element_type=jnp.float32
    )
    att_out = dp_sum(out_grad, order_b).T
    query_grad, key_grad, value_grad = attention_backward(
        query,
        key,
        value,
        segments,
        logsum,
        attended_grad_low.reshape(seqs, length, heads, HEAD_DIM),
        scale,
    )
    mixed_grad = jnp.concatenate(
        [
            part.astype(jnp.bfloat16).reshape(total, local_width)
            for part in (query_grad, key_grad, value_grad)
        ],
        axis=1,
    )
    mixed_flat = to_natural(mixed_grad)
    normed_one_grad = sum_to_owner(times_transposed(qkv_flat), mixed_flat)
    qkv_grad = lax.dot_general(
        full_a, mixed_flat, (((0,), (0,)), ((), ())), preferred_element_type=jnp.float32
    )
    half = 3 * local_width // 2
    att_qkv = jnp.concatenate(
        [dp_sum(qkv_grad[:, :half], order_a), dp_sum(qkv_grad[:, half:], order_b)], axis=1
    ).reshape(shard, 3, local_width)
    mixed_bias = jnp.sum(mixed_flat, axis=0, dtype=jnp.float32)
    bias_qv_part = jnp.stack([mixed_bias[:local_width], mixed_bias[2 * local_width :]])
    norm_one_out, norm_one_back = jax.vjp(layer_norm, rows_in, gains[0], shifts[0])
    input_part, gain_one_grad, shift_one_grad = norm_one_back(normed_one_grad)
    input_grad = (middle_grad + input_part).astype(jnp.bfloat16)
    norm_parts = jnp.stack(
        [
            gain_one_grad,
            gain_two_grad,
            shift_one_grad,
            jnp.sum(branch_low, axis=0, dtype=jnp.float32),
            shift_two_grad,
            jnp.sum(grad_rows, axis=0),
        ]
    )
    groups = lax.axis_size("dp")
    width = norm_parts.shape[1] // (groups * ranks)
    norm_packed = norm_parts.reshape(6, groups, ranks, width).transpose(1, 2, 0, 3)
    norm_packed = norm_packed.reshape(groups, ranks, 6 * width)
    bias_packed = jnp.concatenate(
        [
            bias_qv_part.reshape(2, groups, -1).transpose(1, 0, 2).reshape(groups, -1),
            bias_in_part.reshape(groups, -1),
        ],
        axis=1,
    )
    mine = jnp.arange(ranks, dtype=jnp.int32)[None, :, None] == my_rank
    bias_spread = jnp.where(mine, bias_packed[:, None, :], 0.0)
    packed = jnp.concatenate([norm_packed, bias_spread], axis=2)
    packed = packed.transpose(1, 0, 2)
    rank_bits = list(range(ranks.bit_length() - 1))
    summed = halving_sum(packed, "tensor", rank_bits, jnp.float32)[0]
    summed = halving_sum(summed, "dp", order_a, jnp.float32)[0]
    norm_sums = summed[: 6 * width].reshape(6, width)
    gains_grad, shifts_grad = norm_sums[:2], norm_sums[2:]
    qv_width = bias_qv_part.shape[1] // groups
    att_bias = summed[6 * width : 6 * width + 2 * qv_width].reshape(2, qv_width)
    ff_bias = summed[6 * width + 2 * qv_width :]
    return (
        output,
        input_grad,
        gains_grad,
        shifts_grad,
        att_qkv,
        att_bias,
        att_out,
        ff_in,
        ff_bias,
        ff_down,
    )


def solution(mesh):
    placed = (
        P(("dp", "tensor"), None),
        P(),
        P(),
        P("dp", None, "tensor"),
        P(None, "tensor"),
        P("tensor", "dp"),
        P("dp", "tensor"),
        P("tensor"),
        P("tensor", "dp"),
        P("dp", None),
        P(("dp", "tensor"), None),
    )
    return jax.shard_map(
        per_device,
        mesh=mesh,
        in_specs=placed,
        out_specs=(
            P(("dp", "tensor"), None),
            P(("dp", "tensor"), None),
            P(None, ("dp", "tensor")),
            P(None, ("dp", "tensor")),
            P("dp", None, "tensor"),
            P(None, ("tensor", "dp")),
            P("tensor", "dp"),
            P("dp", "tensor"),
            P(("tensor", "dp")),
            P("tensor", "dp"),
        ),
        check_vma=False,
    )
```
